512 devices in a mesh: ctx: 32 (over x, y, core), head: 16 (over z).
Axes of the slice: x: 4, y: 4, z: 16, core: 2. Of those that a mesh axis runs over, the one named last changes fastest.
Arguments:
- queries: bfloat16 [65536, 2048], P(('ctx', 'head')), may hold values from -6 to 6
- keys_base: bfloat16 [65536, 2048], P(('ctx', 'head')), may hold values from -6 to 6
- values_base: bfloat16 [65536, 2048], P(('ctx', 'head')), may hold values from -6 to 6
- grad_out: bfloat16 [65536, 2048], P(('ctx', 'head')), may hold values from -6 to 6
- key_dir: float32 [2048], replicated, may hold values from -3 to 3
- value_dir: float32 [2048], replicated, may hold values from -6 to 6
- rewards: int32 [65536], P(('ctx', 'head')), may hold values from -1000 to 1000
- episode_end: int32 [65536], P(('ctx', 'head')), may hold values 0 or 1
Outputs:
- attended: bfloat16 [65536, 2048], P(('ctx', 'head'))
- grad_queries: bfloat16 [65536, 2048], P(('ctx', 'head'))
- grad_keys: bfloat16 [65536, 2048], P(('ctx', 'head'))
- grad_values: bfloat16 [65536, 2048], P(('ctx', 'head'))
The draws below stay inside these ranges and needn't reach their ends.
All inputs are finite; a program needn't handle non-finite values. No bound on the sum of `episode_end` on one device may be relied on, other than what follows from the above.
Results may differ from the reference program's by a relative error of at most 0.023.
Values may be sent and summed in bfloat16 or wider, within the bound.
A program may use at most 64 MiB of HBM per device.

```python
import jax
import jax.numpy as jnp
from jax import lax

HEADS = 16
HEAD_DIM = 128
TOK_DEV = 128
D = 2048
WINDOW = 1024
TOKENS = 65536
N_HEAD = 16


def draw_queries(key, part):
    key = jax.random.fold_in(key, 11)
    base = jnp.clip(jax.random.normal(key, (TOKENS, D)), -4.0, 4.0)
    return base.astype(jnp.bfloat16)


def draw_keys_base(key, part):
    key = jax.random.fold_in(key, 23)
    base = jnp.clip(jax.random.normal(key, (TOKENS, D)), -4.0, 4.0)
    return base.astype(jnp.bfloat16)


def with_ends(entries, key, low, top_value):
    longest = entries.shape.index(max(entries.shape))
    spots = []
    for shift in (0, 1):
        where = [jax.random.randint(jax.random.fold_in(key, axis), (), 0, length) for axis, length in enumerate(entries.shape)]
        where[longest] = (where[longest] + shift) % entries.shape[longest]
        spots.append(tuple(where))
    return entries.at[spots[0]].set(low).at[spots[1]].set(top_value)


def levels(own_key, extent, cuts, low, top_value):
    gain = 1.0
    for axis_at, shards_of in cuts:
        heights = jax.random.uniform(jax.random.fold_in(jax.random.fold_in(own_key, 6), axis_at), (shards_of,), jnp.float32, low / len(cuts), top_value / len(cuts))
        gain = gain * jnp.repeat(jnp.exp(heights), extent[axis_at] // shards_of).reshape((-1,) + (1,) * (len(extent) - 1 - axis_at))
    return gain


def normal_values(rng, dims, deviation, reach, split=(), held_as=jnp.bfloat16):
    entries = jax.random.normal(rng, dims, jnp.float32) * deviation
    if len(split) > 0:
        entries = levels(rng, dims, split, -0.22, 0.18) * entries
    return jnp.clip(entries, min=-reach, max=reach).astype(held_as)


def setup_inputs(seed: int = 0) -> dict:
    keys = jax.random.split(jax.random.key(seed), 9)
    queries = draw_queries(jax.random.fold_in(keys[8], 71), 0)
    keys_base = draw_keys_base(jax.random.fold_in(keys[8], 71), 0)
    values_base = normal_values(keys[2], (TOKENS, D), 1.0, 6.0, ((0, 512),))
    grad_out = normal_values(keys[3], (TOKENS, D), 1.0, 6.0, ((0, 512),))
    key_dir = normal_values(keys[4], (D,), 0.5, 3.0, (), jnp.float32)
    value_dir = normal_values(keys[5], (D,), 1.0, 6.0, (), jnp.float32)
    rewards = with_ends(jax.random.randint(keys[6], (TOKENS,), -1000, 1001), jax.random.fold_in(keys[6], 1), -1000, 1000).astype(jnp.int32)
    episode_end = with_ends((jax.random.randint(keys[7], (TOKENS,), 0, 4 * TOK_DEV * N_HEAD) < 1).astype(jnp.int32), jax.random.fold_in(keys[7], 1), 0, 1)
    return dict(queries=queries, keys_base=keys_base, values_base=values_base, grad_out=grad_out, key_dir=key_dir, value_dir=value_dir, rewards=rewards, episode_end=episode_end)


def reference(queries, keys_base, values_base, grad_out, key_dir, value_dir, rewards, episode_end):
    discount = 1.0 - 1.0 / TOKENS
    reward = rewards.astype(jnp.float32) * 0.001
    keeping = (1 - episode_end).astype(jnp.float32) * jnp.float32(discount)

    def advance(carried, pieces):
        current = pieces[0] + pieces[1] * carried
        return current, current

    _, to_go = lax.scan(advance, jnp.float32(0.0), (reward, keeping), reverse=True)
    rtg_scale = (4 * TOK_DEV * N_HEAD) ** -0.5
    lifted = to_go * rtg_scale
    keys_full = (keys_base.astype(jnp.float32) + lifted[:, None] * key_dir[None, :]).astype(jnp.bfloat16)
    values_full = (values_base.astype(jnp.float32) + lifted[:, None] * value_dir[None, :]).astype(jnp.bfloat16)
    window = WINDOW
    tile = min(512, TOKENS)
    key_span = window + tile
    tiles = TOKENS // tile
    score_scale = HEAD_DIM ** -0.5
    q_all = queries.reshape(TOKENS, HEADS, HEAD_DIM)
    k_all = keys_full.reshape(TOKENS, HEADS, HEAD_DIM)
    v_all = values_full.reshape(TOKENS, HEADS, HEAD_DIM)
    g_all = grad_out.reshape(TOKENS, HEADS, HEAD_DIM)
    front = jnp.zeros((window, HEADS, HEAD_DIM), jnp.bfloat16)
    k_pad = jnp.concatenate((front, k_all), 0)
    v_pad = jnp.concatenate((front, v_all), 0)
    row_pos = jnp.arange(tile)[:, None]
    col_pos = jnp.arange(key_span)[None, :]
    band = (col_pos - row_pos >= 1) & (col_pos - row_pos <= window)

    def query_tile(tile_id):
        first_row = (tile_id * tile).astype(jnp.int32)
        q_tile = lax.dynamic_slice_in_dim(q_all, first_row, tile, 0).astype(jnp.float32)
        g_tile = lax.dynamic_slice_in_dim(g_all, first_row, tile, 0)
        k_tile = lax.dynamic_slice_in_dim(k_pad, first_row, key_span, 0).astype(jnp.float32)
        v_tile = lax.dynamic_slice_in_dim(v_pad, first_row, key_span, 0).astype(jnp.float32)
        allowed = band & (first_row + col_pos >= window)
        scores = jnp.einsum("qhd,khd->hqk", q_tile, k_tile) * score_scale
        masked = jnp.where(allowed[None], scores, -jnp.inf)
        top_score = jnp.max(masked, -1, keepdims=True)
        log_total = top_score + jnp.log(jnp.sum(jnp.exp(masked - top_score), -1, keepdims=True))
        probs = jnp.where(allowed[None], jnp.exp(masked - log_total), 0.0)
        weights = probs.astype(jnp.bfloat16).astype(jnp.float32)
        attended = jnp.einsum("hqk,khd->qhd", weights, v_tile).astype(jnp.bfloat16)
        row_dot = jnp.sum(g_tile.astype(jnp.float32) * attended.astype(jnp.float32), -1)
        pushed = jnp.einsum("qhd,khd->hqk", g_tile.astype(jnp.float32), v_tile)
        slopes = (probs * (pushed - row_dot.T[:, :, None]) * score_scale).astype(jnp.bfloat16)
        grad_q = jnp.einsum("hqk,khd->qhd", slopes.astype(jnp.float32), k_tile).astype(jnp.bfloat16)
        return attended, log_total[..., 0].T, row_dot, grad_q

    attended_t, log_t, dot_t, grad_q_t = lax.map(query_tile, jnp.arange(tiles))
    attended = attended_t.reshape(TOKENS, HEADS, HEAD_DIM)
    log_rows = log_t.reshape(TOKENS, HEADS)
    dot_rows = dot_t.reshape(TOKENS, HEADS)
    grad_q_all = grad_q_t.reshape(TOKENS, HEADS, HEAD_DIM)
    q_pad = jnp.concatenate((q_all, front), 0)
    g_pad = jnp.concatenate((g_all, front), 0)
    extra = jnp.zeros((window, HEADS), jnp.float32)
    log_pad = jnp.concatenate((log_rows, extra), 0)
    dot_pad = jnp.concatenate((dot_rows, extra), 0)
    query_pos = jnp.arange(key_span)[:, None]
    key_pos = jnp.arange(tile)[None, :]
    lag_band = (query_pos - key_pos >= 0) & (query_pos - key_pos <= window - 1)

    def key_tile(tile_id):
        first_row = (tile_id * tile).astype(jnp.int32)
        k_tile = lax.dynamic_slice_in_dim(k_all, first_row, tile, 0).astype(jnp.float32)
        v_tile = lax.dynamic_slice_in_dim(v_all, first_row, tile, 0).astype(jnp.float32)
        q_tile = lax.dynamic_slice_in_dim(q_pad, first_row, key_span, 0).astype(jnp.float32)
        g_tile = lax.dynamic_slice_in_dim(g_pad, first_row, key_span, 0).astype(jnp.float32)
        log_tile = lax.dynamic_slice_in_dim(log_pad, first_row, key_span, 0).T
        dot_tile = lax.dynamic_slice_in_dim(dot_pad, first_row, key_span, 0).T
        allowed = lag_band & (first_row + query_pos < TOKENS)
        scores = jnp.einsum("qhd,khd->hqk", q_tile, k_tile) * score_scale
        probs = jnp.where(allowed[None], jnp.exp(scores - log_tile[:, :, None]), 0.0)
        weights = probs.astype(jnp.bfloat16).astype(jnp.float32)
        pushed = jnp.einsum("qhd,khd->hqk", g_tile, v_tile)
        slopes = (probs * (pushed - dot_tile[:, :, None]) * score_scale).astype(jnp.bfloat16)
        grad_k = jnp.einsum("hqk,qhd->khd", slopes.astype(jnp.float32), q_tile).astype(jnp.bfloat16)
        grad_v = jnp.einsum("hqk,qhd->khd", weights, g_tile).astype(jnp.bfloat16)
        return grad_k, grad_v

    grad_k_t, grad_v_t = lax.map(key_tile, jnp.arange(tiles))
    shape_out = (TOKENS, HEADS * HEAD_DIM)
    return (attended.reshape(shape_out), grad_q_all.reshape(shape_out),
            grad_k_t.reshape(shape_out), grad_v_t.reshape(shape_out))
```

```python
import functools
import math

import jax
import jax.numpy as jnp
from jax import lax
from jax.experimental import pallas as pl
from jax.experimental.pallas import tpu as pltpu
from jax.sharding import PartitionSpec as P

HEAD_DIM = 128
BF16 = jnp.bfloat16
F32 = jnp.float32
MESH = pl.DeviceIdType.MESH
K, V, Q, G = range(4)
O, DQ, DK, DV = range(4)
UP, DOWN = range(2)


def dot_nt(a, b):
    return lax.dot_general(a, b, (((1,), (1,)), ((), ())), preferred_element_type=F32)


def dot_tn(a, b):
    return lax.dot_general(a, b, (((0,), (0,)), ((), ())), preferred_element_type=F32)


def layer(
    n_ctx, n_head, rows, all_rows,
    q_hbm, k_hbm, v_hbm, g_hbm, kdir_ref, vdir_ref, rew_ref, end_ref,
    o_hbm, dq_hbm, dk_hbm, dv_hbm,
    send_in, in_up, in_down, send_out, out_up, out_down,
    kbuf, vbuf, dk_acc, dv_acc, q_in, g_in, grad_send, grad_recv,
    small, suffix, ctx_val, ctx_got,
    load_sem, store_sem, ring_ssem, ring_rsem, halo_ssem, halo_rsem, small_ssem, small_rsem,
):
    c = lax.axis_index("ctx")
    h = lax.axis_index("head")
    half = n_head // 2
    span = (half + 1) * rows
    score_scale = HEAD_DIM ** (-0.5)
    exp_scale = score_scale * math.log2(math.e)

    def at_head(off):
        return (c, lax.rem(h + off + n_head, n_head))

    def at_ctx(off):
        return (lax.rem(c + off + n_ctx, n_ctx), h)

    def load(stream, src):
        for j in range(n_head):
            col = pl.multiple_of(lax.rem(h + j, n_head) * HEAD_DIM, HEAD_DIM)
            pltpu.make_async_copy(
                src.at[:, pl.ds(col, HEAD_DIM)], send_in.at[stream, j], load_sem.at[stream]
            ).start()

    def wait_load(stream):
        pltpu.make_async_copy(send_in.at[stream], send_in.at[stream], load_sem.at[stream]).wait()

    load(K, k_hbm)
    load(V, v_hbm)

    barrier = pltpu.get_barrier_semaphore()
    head_steps = [1 << k for k in range(n_head.bit_length() - 1)]
    ctx_steps = [1 << k for k in range(n_ctx.bit_length() - 1)]
    senders = [at_head(d) for d in [-1] + head_steps] + [at_ctx(d) for d in [-1] + ctx_steps]
    for device in senders:
        pl.semaphore_signal(barrier, inc=1, device_id=device, device_id_type=MESH)
    load(Q, q_hbm)
    load(G, g_hbm)
    dk_acc[...] = jnp.zeros_like(dk_acc)
    dv_acc[...] = jnp.zeros_like(dv_acc)
    pl.semaphore_wait(barrier, len(senders))

    def reach(stream, way):
        return half if (stream + way) % 2 == 0 else half - 1

    bufs = ((send_in, in_up, in_down), (send_out, out_up, out_down))

    def ring(phase, stream, way, step):
        far = reach(stream, way)
        count = far - step + 1
        send, up, down = bufs[phase]
        if way == UP:
            store, first = up, step - 1
            src = send.at[stream, pl.ds(1, far)] if step == 1 else up.at[stream, step - 2, pl.ds(first, count)]
        else:
            store, first = down, half - far
            src = (
                send.at[stream, pl.ds(n_head - far, far)]
                if step == 1
                else down.at[stream, step - 2, pl.ds(first, count)]
            )
        return pltpu.make_async_remote_copy(
            src_ref=src,
            dst_ref=store.at[stream, step - 1, pl.ds(first, count)],
            send_sem=ring_ssem.at[phase, way, stream, step - 1],
            recv_sem=ring_rsem.at[phase, way, stream, step - 1],
            device_id=at_head(1 if way == UP else -1),
            device_id_type=MESH,
        )

    def ring_start(phase, stream):
        for way in (UP, DOWN):
            ring(phase, stream, way, 1).start()

    def ring_step(phase, stream, step):
        for way in (UP, DOWN):
            if step <= reach(stream, way):
                ring(phase, stream, way, step).wait_recv()
                if step < reach(stream, way):
                    ring(phase, stream, way, step + 1).start()

    def arrived(phase, stream, way, step):
        if way == UP:
            return bufs[phase][1].at[stream, step - 1, step - 1]
        return bufs[phase][2].at[stream, step - 1, half - step]

    def far_way(stream):
        return UP if reach(stream, UP) == half else DOWN

    wait_load(K)
    ring_start(0, K)
    wait_load(V)
    ring_start(0, V)

    lane = lax.broadcasted_iota(jnp.int32, (8, rows), 1)
    row = lax.broadcasted_iota(jnp.int32, (8, rows), 0)
    keep = jnp.broadcast_to((1 - end_ref[...]).astype(F32) * F32(1.0 - 1.0 / all_rows), (8, rows))
    total = jnp.broadcast_to(rew_ref[...].astype(F32) * 0.001, (8, rows))
    for k in range(rows.bit_length() - 1):
        d = 1 << k
        inside = lane < rows - d
        later_keep = jnp.where(inside, pltpu.roll(keep, rows - d, 1), 1.0)
        later_total = jnp.where(inside, pltpu.roll(total, rows - d, 1), 0.0)
        total = total + keep * later_total
        keep = keep * later_keep
    small[0] = jnp.where(row == 0, total, keep)

    def head_copy(k):
        d = head_steps[k]
        return pltpu.make_async_remote_copy(
            src_ref=small.at[pl.ds(0, d)], dst_ref=small.at[pl.ds(d, d)],
            send_sem=small_ssem.at[k], recv_sem=small_rsem.at[k],
            device_id=at_head(-d), device_id_type=MESH,
        )

    n_small = len(head_steps)
    ctx_moves = [1] + ctx_steps

    def ctx_copy(k):
        return pltpu.make_async_remote_copy(
            src_ref=ctx_val.at[k], dst_ref=ctx_got.at[k],
            send_sem=small_ssem.at[n_small + k], recv_sem=small_rsem.at[n_small + k],
            device_id=at_ctx(-ctx_moves[k]), device_id_type=MESH,
        )

    def splat(ref, index, which):
        return jnp.broadcast_to(ref[index, which : which + 1, 0:1], (1, rows))

    def pair(total_row, keep_row):
        return jnp.where(row == 0, total_row, keep_row)

    def head_move(k):
        head_copy(k).wait_recv()
        if k + 1 < n_small:
            head_copy(k + 1).start()
            return
        after_total, after_keep = jnp.zeros((1, rows), F32), jnp.ones((1, rows), F32)
        for z in reversed(range(n_head)):
            suffix[z] = pair(after_total, after_keep)
            slot = lax.rem(z - h + n_head, n_head)
            z_total, z_keep = splat(small, slot, 0), splat(small, slot, 1)
            after_total = z_total + z_keep * after_total
            after_keep = z_keep * after_keep
        ctx_val[0] = pair(after_total, after_keep)
        ctx_copy(0).start()

    def ctx_move(k):
        ctx_copy(k).wait_recv()
        d = ctx_moves[k]
        got = ctx_got[k]
        ahead = c + d + (0 if k == 0 else 1)
        valid = jnp.broadcast_to(ahead, (8, rows)) < n_ctx
        got_total = jnp.where(valid, jnp.broadcast_to(got[0:1], (8, rows)), 0.0)
        got_keep = jnp.where(valid, jnp.broadcast_to(got[1:2], (8, rows)), 1.0)
        if k == 0:
            ctx_val[1] = jnp.where(row == 0, got_total, got_keep)
        else:
            mine = ctx_val[k]
            my_total = jnp.broadcast_to(mine[0:1], (8, rows))
            my_keep = jnp.broadcast_to(mine[1:2], (8, rows))
            ctx_val[k + 1] = jnp.where(row == 0, my_total + my_keep * got_total, my_keep * got_keep)
        if k + 1 < len(ctx_moves):
            ctx_copy(k + 1).start()

    head_copy(0).start()
    moves = [functools.partial(head_move, k) for k in range(n_small)]
    moves += [functools.partial(ctx_move, k) for k in range(len(ctx_moves))]

    def finish(j, k_raw, v_raw):
        z = lax.rem(h + j, n_head)
        carry = ctx_val[len(ctx_moves), 0:1]
        carry_z = suffix[z, 0:1] + suffix[z, 1:2] * carry
        to_go = small[j, 0:1] + small[j, 1:2] * carry_z
        lifted = to_go * (4 * rows * n_head) ** (-0.5)
        column = jnp.broadcast_to(lifted, (rows, rows)).T
        place = pl.ds(pl.multiple_of((half + z) * rows, rows), rows)
        kbuf[place, :] = (k_raw[...].astype(F32) + column * kdir_ref[pl.ds(h, 1), :]).astype(BF16)
        vbuf[place, :] = (v_raw[...].astype(F32) + column * vdir_ref[pl.ds(h, 1), :]).astype(BF16)

    def finish_step(step):
        if step == 0:
            finish(0, send_in.at[K, 0], send_in.at[V, 0])
        elif step < half:
            finish(n_head - step, arrived(0, K, UP, step), arrived(0, V, UP, step))
            finish(step, arrived(0, K, DOWN, step), arrived(0, V, DOWN, step))
        else:
            finish(half, arrived(0, K, far_way(K), half), arrived(0, V, far_way(V), half))

    per_step = (3, 3, 2, 2)
    q_start = half - 3
    for step in range(1, half + 1):
        if moves:
            for move in moves[: per_step[step - 1]]:
                move()
            moves = moves[per_step[step - 1] :]
        ring_step(0, K, step)
        ring_step(0, V, step)
        if step == q_start:
            wait_load(Q)
            ring_start(0, Q)
            wait_load(G)
            ring_start(0, G)
        if step == len(per_step):
            for done in range(step + 1):
                finish_step(done)
        elif step > len(per_step):
            finish_step(step)

    def halo(which):
        buf = (kbuf, vbuf)[which]
        return pltpu.make_async_remote_copy(
            src_ref=buf.at[pl.ds(n_head * rows, half * rows)], dst_ref=buf.at[pl.ds(0, half * rows)],
            send_sem=halo_ssem.at[which], recv_sem=halo_rsem.at[which],
            device_id=at_ctx(1), device_id_type=MESH,
        )

    halo(0).start()
    halo(1).start()
    q_in[0] = send_in[Q, 0]
    g_in[0] = send_in[G, 0]
    halo(0).wait_recv()
    halo(1).wait_recv()

    def take(step):
        ring_step(0, Q, step)
        ring_step(0, G, step)
        up, down = (UP, DOWN) if step < half else (far_way(Q), far_way(G))
        if step < half:
            q_in[2 * step - 1] = arrived(0, Q, UP, step)[...]
            g_in[2 * step - 1] = arrived(0, G, UP, step)[...]
            q_in[2 * step] = arrived(0, Q, DOWN, step)[...]
            g_in[2 * step] = arrived(0, G, DOWN, step)[...]
        else:
            q_in[2 * step - 1] = arrived(0, Q, up, step)[...]
            g_in[2 * step - 1] = arrived(0, G, down, step)[...]

    def tile(it, carry):
        for step in range(1, half + 1):
            pl.when(it == 2 * step - 1)(functools.partial(take, step))
        odd = lax.rem(it, 2)
        j = odd * (n_head - (it + 1) // 2) + (1 - odd) * (it // 2)
        t = lax.rem(h + j, n_head)
        place = pl.ds(pl.multiple_of(t * rows, rows), span)
        q, g, k, v = q_in[it], g_in[it], kbuf[place, :], vbuf[place, :]
        key = lax.broadcasted_iota(jnp.int32, (span, rows), 0)
        query = lax.broadcasted_iota(jnp.int32, (span, rows), 1)
        before = jnp.where(c == 0, half * rows - t * rows, 0)
        allowed = (key >= jnp.maximum(query + 1, before)) & (key <= query + half * rows)
        s = jnp.where(allowed, dot_nt(k, q), -1e30)
        top = jnp.max(s, axis=0, keepdims=True)
        e = jnp.exp2((s - top) * exp_scale)
        probs = e * (1.0 / jnp.sum(e, axis=0, keepdims=True))
        weights = probs.astype(BF16)
        attended = dot_tn(weights, v).astype(BF16)
        row_dot = jnp.sum((attended.astype(F32) * g.astype(F32)).T, axis=0, keepdims=True)
        slopes = (probs * (dot_nt(v, g) - row_dot) * score_scale).astype(BF16)
        send_out[O, j] = attended
        send_out[DQ, j] = dot_tn(slopes, k).astype(BF16)
        dk_acc[place, :] += jnp.dot(slopes, q, preferred_element_type=F32)
        dv_acc[place, :] += jnp.dot(weights, g, preferred_element_type=F32)
        return carry

    lax.fori_loop(0, n_head, tile, 0)

    ring_start(1, O)
    ring_start(1, DQ)

    grad_send[0] = dk_acc[pl.ds(0, half * rows), :].astype(BF16)
    grad_send[1] = dv_acc[pl.ds(0, half * rows), :].astype(BF16)

    def grad(which):
        return pltpu.make_async_remote_copy(
            src_ref=grad_send.at[which], dst_ref=grad_recv.at[which],
            send_sem=halo_ssem.at[2 + which], recv_sem=halo_rsem.at[2 + which],
            device_id=at_ctx(-1), device_id_type=MESH,
        )

    grad(0).start()
    grad(1).start()
    for z in range(n_head):
        j = lax.rem(z - h + n_head, n_head)
        if z == half:
            grad(0).wait_recv()
            grad(1).wait_recv()
        dk = dk_acc[pl.ds((half + z) * rows, rows), :]
        dv = dv_acc[pl.ds((half + z) * rows, rows), :]
        if z >= half:
            dk = dk + grad_recv[0, pl.ds((z - half) * rows, rows), :].astype(F32)
            dv = dv + grad_recv[1, pl.ds((z - half) * rows, rows), :].astype(F32)
        send_out[DK, j] = dk.astype(BF16)
        send_out[DV, j] = dv.astype(BF16)
    ring_start(1, DK)
    ring_start(1, DV)

    outs = (o_hbm, dq_hbm, dk_hbm, dv_hbm)

    def store(stream, j, src):
        col = pl.multiple_of(lax.rem(h + j, n_head) * HEAD_DIM, HEAD_DIM)
        pltpu.make_async_copy(
            src, outs[stream].at[:, pl.ds(col, HEAD_DIM)], store_sem.at[stream, j]
        ).start()

    for stream in range(4):
        store(stream, 0, send_out.at[stream, 0])
    for step in range(1, half + 1):
        for stream in range(4):
            ring_step(1, stream, step)
            if step < half:
                store(stream, n_head - step, arrived(1, stream, UP, step))
                store(stream, step, arrived(1, stream, DOWN, step))
            else:
                store(stream, half, arrived(1, stream, far_way(stream), half))

    for phase in range(2):
        for stream in range(4):
            for way in (UP, DOWN):
                for step in range(1, reach(stream, way) + 1):
                    ring(phase, stream, way, step).wait_send()
    for k in range(n_small):
        head_copy(k).wait_send()
    for k in range(len(ctx_moves)):
        ctx_copy(k).wait_send()
    for which in range(2):
        halo(which).wait_send()
        grad(which).wait_send()
    for stream in range(4):
        for j in range(n_head):
            pltpu.make_async_copy(
                send_out.at[stream, 0], outs[stream].at[:, pl.ds(0, HEAD_DIM)], store_sem.at[stream, j]
            ).wait()


def on_device(queries, keys_base, values_base, grad_out, key_dir, value_dir, rewards, episode_end):
    rows, features = queries.shape
    n_ctx, n_head = lax.axis_size("ctx"), lax.axis_size("head")
    half = n_head // 2
    all_rows = rows * n_ctx * n_head
    unit = (rows, HEAD_DIM)
    n_small = (n_head.bit_length() - 1) + n_ctx.bit_length()
    ctx_moves = n_ctx.bit_length()
    hbm = pl.BlockSpec(memory_space=pl.ANY)
    vmem = pl.BlockSpec(memory_space=pltpu.VMEM)
    dma = pltpu.SemaphoreType.DMA
    return pl.pallas_call(
        functools.partial(layer, n_ctx, n_head, rows, all_rows),
        out_shape=[jax.ShapeDtypeStruct((rows, features), BF16)] * 4,
        in_specs=[hbm] * 4 + [vmem] * 4,
        out_specs=[hbm] * 4,
        scratch_shapes=[
            pltpu.VMEM((4, n_head) + unit, BF16),
            pltpu.VMEM((4, half, half) + unit, BF16),
            pltpu.VMEM((4, half, half) + unit, BF16),
            pltpu.VMEM((4, n_head) + unit, BF16),
            pltpu.VMEM((4, half, half) + unit, BF16),
            pltpu.VMEM((4, half, half) + unit, BF16),
            pltpu.VMEM(((n_head + half) * rows, HEAD_DIM), BF16),
            pltpu.VMEM(((n_head + half) * rows, HEAD_DIM), BF16),
            pltpu.VMEM(((n_head + half) * rows, HEAD_DIM), F32),
            pltpu.VMEM(((n_head + half) * rows, HEAD_DIM), F32),
            pltpu.VMEM((n_head,) + unit, BF16),
            pltpu.VMEM((n_head,) + unit, BF16),
            pltpu.VMEM((2, half * rows, HEAD_DIM), BF16),
            pltpu.VMEM((2, half * rows, HEAD_DIM), BF16),
            pltpu.VMEM((n_head, 8, rows), F32),
            pltpu.VMEM((n_head, 8, rows), F32),
            pltpu.VMEM((ctx_moves + 1, 8, rows), F32),
            pltpu.VMEM((ctx_moves, 8, rows), F32),
            dma((4,)),
            dma((4, n_head)),
            dma((2, 2, 4, half)),
            dma((2, 2, 4, half)),
            dma((4,)),
            dma((4,)),
            dma((n_small,)),
            dma((n_small,)),
        ],
        compiler_params=pltpu.CompilerParams(
            collective_id=0, has_side_effects=True, vmem_limit_bytes=56 * 2**20
        ),
    )(
        queries, keys_base, values_base, grad_out,
        key_dir.reshape(n_head, HEAD_DIM), value_dir.reshape(n_head, HEAD_DIM),
        rewards.reshape(1, rows), episode_end.reshape(1, rows),
    )


def solution(mesh):
    wide = P(("ctx", "head"), None)
    steps = P(("ctx", "head"))
    return jax.shard_map(
        on_device,
        mesh=mesh,
        in_specs=(wide, wide, wide, wide, P(), P(), steps, steps),
        out_specs=(wide, wide, wide, wide),
        check_vma=False,
    )
```

```python
import functools
import math

import jax
import jax.numpy as jnp
from jax import lax
from jax.experimental import pallas as pl
from jax.experimental.pallas import tpu as pltpu
from jax.sharding import PartitionSpec as P

HEAD_DIM = 128
BF16 = jnp.bfloat16
F32 = jnp.float32
MESH = pl.DeviceIdType.MESH
K, V, Q, G = range(4)
O, DQ, DK, DV = range(4)
LAG = 0


def dot_nt(a, b):
    return lax.dot_general(a, b, (((1,), (1,)), ((), ())), preferred_element_type=F32)


def dot_tn(a, b):
    return lax.dot_general(a, b, (((0,), (0,)), ((), ())), preferred_element_type=F32)


def layer(
    n_ctx, n_head, rows, all_rows,
    q_hbm, k_hbm, v_hbm, g_hbm, kdir_ref, vdir_ref, rew_ref, end_ref,
    o_hbm, dq_hbm, dk_hbm, dv_hbm,
    got, sent, kbuf, vbuf, dk_acc, dv_acc, grad_send, grad_recv, small, suffix, ctx_val, ctx_got,
    own_sem, in_ssem, in_rsem, out_ssem, out_rsem,
    halo_ssem, halo_rsem, small_ssem, small_rsem, ctx_ssem, ctx_rsem,
):
    c = lax.axis_index("ctx")
    h = lax.axis_index("head")
    half = n_head // 2
    span = (half + 1) * rows
    score_scale = HEAD_DIM ** (-0.5)
    exp_scale = score_scale * math.log2(math.e)
    ins = (k_hbm, v_hbm, q_hbm, g_hbm)
    outs = (o_hbm, dq_hbm, dk_hbm, dv_hbm)
    around = [(d, n_head - d)[way] for d in range(1, half) for way in range(2)] + [half]

    def head_at(off):
        return lax.rem(h + off, n_head)

    def at_ctx(off):
        return (lax.rem(c + off + n_ctx, n_ctx), h)

    def columns(off):
        return pl.ds(pl.multiple_of(head_at(off) * HEAD_DIM, HEAD_DIM), HEAD_DIM)

    def own_in(a):
        return pltpu.make_async_copy(ins[a].at[:, columns(0)], got.at[a, 0], own_sem.at[0, a])

    def own_out(a):
        return pltpu.make_async_copy(sent.at[a, 0], outs[a].at[:, columns(0)], own_sem.at[1, a])

    def send_in(a, j):
        return pltpu.make_async_remote_copy(
            src_ref=ins[a].at[:, columns(j)], dst_ref=got.at[a, n_head - j],
            send_sem=in_ssem.at[a, j], recv_sem=in_rsem.at[a, n_head - j],
            device_id=(c, head_at(j)), device_id_type=MESH,
        )

    def receive_in(a, j):
        return pltpu.make_async_remote_copy(
            src_ref=ins[a].at[:, columns(j)], dst_ref=got.at[a, j],
            send_sem=in_ssem.at[a, j], recv_sem=in_rsem.at[a, j],
            device_id=(c, head_at(j)), device_id_type=MESH,
        )

    def send_out(a, j):
        return pltpu.make_async_remote_copy(
            src_ref=sent.at[a, j], dst_ref=outs[a].at[:, columns(0)],
            send_sem=out_ssem.at[a, j], recv_sem=out_rsem.at[a, n_head - j],
            device_id=(c, head_at(j)), device_id_type=MESH,
        )

    def receive_out(a, j):
        return pltpu.make_async_remote_copy(
            src_ref=sent.at[a, j], dst_ref=outs[a].at[:, columns(j)],
            send_sem=out_ssem.at[a, j], recv_sem=out_rsem.at[a, j],
            device_id=(c, head_at(j)), device_id_type=MESH,
        )

    barrier = pltpu.get_barrier_semaphore()
    ctx_steps = [1 << k for k in range(n_ctx.bit_length() - 1)]
    senders = [(c, head_at(j)) for j in around] + [at_ctx(d) for d in [-1] + ctx_steps]
    for device in senders:
        pl.semaphore_signal(barrier, inc=1, device_id=device, device_id_type=MESH)
    for a in range(4):
        own_in(a).start()
    dk_acc[...] = jnp.zeros_like(dk_acc)
    dv_acc[...] = jnp.zeros_like(dv_acc)

    lane = lax.broadcasted_iota(jnp.int32, (8, rows), 1)
    row = lax.broadcasted_iota(jnp.int32, (8, rows), 0)
    keep = jnp.broadcast_to((1 - end_ref[...]).astype(F32) * F32(1.0 - 1.0 / all_rows), (8, rows))
    total = jnp.broadcast_to(rew_ref[...].astype(F32) * 0.001, (8, rows))
    for k in range(rows.bit_length() - 1):
        d = 1 << k
        inside = lane < rows - d
        later_keep = jnp.where(inside, pltpu.roll(keep, rows - d, 1), 1.0)
        later_total = jnp.where(inside, pltpu.roll(total, rows - d, 1), 0.0)
        total = total + keep * later_total
        keep = keep * later_keep
    small[0] = jnp.where(row == 0, total, keep)
    pl.semaphore_wait(barrier, len(senders))

    def send_small(j):
        return pltpu.make_async_remote_copy(
            src_ref=small.at[0], dst_ref=small.at[n_head - j],
            send_sem=small_ssem.at[j], recv_sem=small_rsem.at[n_head - j],
            device_id=(c, head_at(j)), device_id_type=MESH,
        )

    def receive_small(j):
        return pltpu.make_async_remote_copy(
            src_ref=small.at[0], dst_ref=small.at[j],
            send_sem=small_ssem.at[j], recv_sem=small_rsem.at[j],
            device_id=(c, head_at(j)), device_id_type=MESH,
        )

    for j in around:
        send_small(j).start()
    for j in around:
        send_in(K, j).start()
        send_in(V, j).start()

    ctx_moves = [1] + ctx_steps

    def ctx_copy(k):
        return pltpu.make_async_remote_copy(
            src_ref=ctx_val.at[k], dst_ref=ctx_got.at[k],
            send_sem=ctx_ssem.at[k], recv_sem=ctx_rsem.at[k],
            device_id=at_ctx(-ctx_moves[k]), device_id_type=MESH,
        )

    def splat(ref, index, which):
        return jnp.broadcast_to(ref[index, which : which + 1, 0:1], (1, rows))

    def pair(total_row, keep_row):
        return jnp.where(row == 0, total_row, keep_row)

    for j in around:
        receive_small(j).wait_recv()
    after_total, after_keep = jnp.zeros((1, rows), F32), jnp.ones((1, rows), F32)
    for z in reversed(range(n_head)):
        suffix[z] = pair(after_total, after_keep)
        slot = lax.rem(z - h + n_head, n_head)
        z_total, z_keep = splat(small, slot, 0), splat(small, slot, 1)
        after_total = z_total + z_keep * after_total
        after_keep = z_keep * after_keep
    ctx_val[0] = pair(after_total, after_keep)
    ctx_copy(0).start()
    for k, d in enumerate(ctx_moves):
        ctx_copy(k).wait_recv()
        theirs, mine = ctx_got[k], ctx_val[k]
        ahead = c + d + (0 if k == 0 else 1)
        valid = jnp.broadcast_to(ahead, (8, rows)) < n_ctx
        got_total = jnp.where(valid, jnp.broadcast_to(theirs[0:1], (8, rows)), 0.0)
        got_keep = jnp.where(valid, jnp.broadcast_to(theirs[1:2], (8, rows)), 1.0)
        if k > 0:
            my_total = jnp.broadcast_to(mine[0:1], (8, rows))
            my_keep = jnp.broadcast_to(mine[1:2], (8, rows))
            got_total, got_keep = my_total + my_keep * got_total, my_keep * got_keep
        ctx_val[k + 1] = jnp.where(row == 0, got_total, got_keep)
        if k + 1 < len(ctx_moves):
            ctx_copy(k + 1).start()

    def finish(j):
        z = head_at(j)
        carry = ctx_val[len(ctx_moves), 0:1]
        carry_z = suffix[z, 0:1] + suffix[z, 1:2] * carry
        to_go = small[j, 0:1] + small[j, 1:2] * carry_z
        lifted = to_go * (4 * rows * n_head) ** (-0.5)
        column = jnp.broadcast_to(lifted, (rows, rows)).T
        place = pl.ds(pl.multiple_of((half + z) * rows, rows), rows)
        kbuf[place, :] = (got[K, j].astype(F32) + column * kdir_ref[pl.ds(h, 1), :]).astype(BF16)
        vbuf[place, :] = (got[V, j].astype(F32) + column * vdir_ref[pl.ds(h, 1), :]).astype(BF16)

    own_in(K).wait()
    own_in(V).wait()
    finish(0)
    for at, j in enumerate(around):
        receive_in(K, j).wait_recv()
        receive_in(V, j).wait_recv()
        finish(j)
        if at >= LAG:
            send_in(Q, around[at - LAG]).start()
            send_in(G, around[at - LAG]).start()
    for j in around[len(around) - LAG :]:
        send_in(Q, j).start()
        send_in(G, j).start()

    def halo(which):
        buf = (kbuf, vbuf)[which]
        return pltpu.make_async_remote_copy(
            src_ref=buf.at[pl.ds(n_head * rows, half * rows)], dst_ref=buf.at[pl.ds(0, half * rows)],
            send_sem=halo_ssem.at[which], recv_sem=halo_rsem.at[which],
            device_id=at_ctx(1), device_id_type=MESH,
        )

    halo(0).start()
    halo(1).start()
    own_in(Q).wait()
    own_in(G).wait()
    halo(0).wait_recv()
    halo(1).wait_recv()

    def slot_of(it):
        odd = lax.rem(it, 2)
        return odd * (n_head - (it + 1) // 2) + (1 - odd) * (it // 2)

    def tile(it, carry):
        j = slot_of(it)

        @pl.when(it > 0)
        def _():
            receive_in(Q, j).wait_recv()
            receive_in(G, j).wait_recv()

        t = head_at(j)
        place = pl.ds(pl.multiple_of(t * rows, rows), span)
        q, g, k, v = got[Q, j], got[G, j], kbuf[place, :], vbuf[place, :]
        key = lax.broadcasted_iota(jnp.int32, (span, rows), 0)
        query = lax.broadcasted_iota(jnp.int32, (span, rows), 1)
        before = jnp.where(c == 0, half * rows - t * rows, 0)
        allowed = (key >= jnp.maximum(query + 1, before)) & (key <= query + half * rows)
        s = jnp.where(allowed, dot_nt(k, q), -1e30)
        top = jnp.max(s, axis=0, keepdims=True)
        e = jnp.exp2((s - top) * exp_scale)
        probs = e * (1.0 / jnp.sum(e, axis=0, keepdims=True))
        weights = probs.astype(BF16)
        attended = dot_tn(weights, v).astype(BF16)
        row_dot = jnp.sum((attended.astype(F32) * g.astype(F32)).T, axis=0, keepdims=True)
        slopes = (probs * (dot_nt(v, g) - row_dot) * score_scale).astype(BF16)
        sent[O, j] = attended
        sent[DQ, j] = dot_tn(slopes, k).astype(BF16)

        @pl.when(it > 0)
        def _():
            send_out(O, j).start()
            send_out(DQ, j).start()

        dk_acc[place, :] += jnp.dot(slopes, q, preferred_element_type=F32)
        dv_acc[place, :] += jnp.dot(weights, g, preferred_element_type=F32)
        return carry

    lax.fori_loop(0, n_head, tile, 0)

    grad_send[0] = dk_acc[pl.ds(0, half * rows), :].astype(BF16)
    grad_send[1] = dv_acc[pl.ds(0, half * rows), :].astype(BF16)

    def grad(which):
        return pltpu.make_async_remote_copy(
            src_ref=grad_send.at[which], dst_ref=grad_recv.at[which],
            send_sem=halo_ssem.at[2 + which], recv_sem=halo_rsem.at[2 + which],
            device_id=at_ctx(-1), device_id_type=MESH,
        )

    grad(0).start()
    grad(1).start()
    own_out(O).start()
    own_out(DQ).start()
    grad(0).wait_recv()
    grad(1).wait_recv()

    def collect(it, carry):
        j = slot_of(it)
        z = head_at(j)
        place = pl.ds(pl.multiple_of((half + z) * rows, rows), rows)
        back = pl.ds(pl.multiple_of(jnp.maximum(z - half, 0) * rows, rows), rows)
        for which, acc in enumerate((dk_acc, dv_acc)):
            returned = jnp.where(z >= half, grad_recv[which, back, :].astype(F32), 0.0)
            sent[DK + which, j] = (acc[place, :] + returned).astype(BF16)

        @pl.when(it > 0)
        def _():
            send_out(DK, j).start()
            send_out(DV, j).start()

        return carry

    lax.fori_loop(0, n_head, collect, 0)
    own_out(DK).start()
    own_out(DV).start()

    for j in around:
        send_small(j).wait_send()
    for k in range(len(ctx_moves)):
        ctx_copy(k).wait_send()
    for which in range(2):
        halo(which).wait_send()
        grad(which).wait_send()
    for a in range(4):
        own_out(a).wait()
        for j in around:
            send_in(a, j).wait_send()
            send_out(a, j).wait_send()
            receive_out(a, j).wait_recv()


def on_device(queries, keys_base, values_base, grad_out, key_dir, value_dir, rewards, episode_end):
    rows, features = queries.shape
    n_ctx, n_head = lax.axis_size("ctx"), lax.axis_size("head")
    half = n_head // 2
    all_rows = rows * n_ctx * n_head
    unit = (rows, HEAD_DIM)
    ctx_moves = n_ctx.bit_length()
    hbm = pl.BlockSpec(memory_space=pl.ANY)
    vmem = pl.BlockSpec(memory_space=pltpu.VMEM)
    dma = pltpu.SemaphoreType.DMA
    return pl.pallas_call(
        functools.partial(layer, n_ctx, n_head, rows, all_rows),
        out_shape=[jax.ShapeDtypeStruct((rows, features), BF16)] * 4,
        in_specs=[hbm] * 4 + [vmem] * 4,
        out_specs=[hbm] * 4,
        scratch_shapes=[
            pltpu.VMEM((4, n_head) + unit, BF16),
            pltpu.VMEM((4, n_head) + unit, BF16),
            pltpu.VMEM(((n_head + half) * rows, HEAD_DIM), BF16),
            pltpu.VMEM(((n_head + half) * rows, HEAD_DIM), BF16),
            pltpu.VMEM(((n_head + half) * rows, HEAD_DIM), F32),
            pltpu.VMEM(((n_head + half) * rows, HEAD_DIM), F32),
            pltpu.VMEM((2, half * rows, HEAD_DIM), BF16),
            pltpu.VMEM((2, half * rows, HEAD_DIM), BF16),
            pltpu.VMEM((n_head, 8, rows), F32),
            pltpu.VMEM((n_head, 8, rows), F32),
            pltpu.VMEM((ctx_moves + 1, 8, rows), F32),
            pltpu.VMEM((ctx_moves, 8, rows), F32),
            dma((2, 4)),
            dma((4, n_head)),
            dma((4, n_head)),
            dma((4, n_head)),
            dma((4, n_head)),
            dma((4,)),
            dma((4,)),
            dma((n_head,)),
            dma((n_head,)),
            dma((ctx_moves,)),
            dma((ctx_moves,)),
        ],
        compiler_params=pltpu.CompilerParams(
            collective_id=0, has_side_effects=True, vmem_limit_bytes=48 * 2**20
        ),
    )(
        queries, keys_base, values_base, grad_out,
        key_dir.reshape(n_head, HEAD_DIM), value_dir.reshape(n_head, HEAD_DIM),
        rewards.reshape(1, rows), episode_end.reshape(1, rows),
    )


def solution(mesh):
    wide = P(("ctx", "head"), None)
    steps = P(("ctx", "head"))
    return jax.shard_map(
        on_device,
        mesh=mesh,
        in_specs=(wide, wide, wide, wide, P(), P(), steps, steps),
        out_specs=(wide, wide, wide, wide),
        check_vma=False,
    )
```

```python
import functools
import math

import jax
import jax.numpy as jnp
from jax import lax
from jax.experimental import pallas as pl
from jax.experimental.pallas import tpu as pltpu
from jax.sharding import PartitionSpec as P

HEAD_DIM = 128
BF16 = jnp.bfloat16
F32 = jnp.float32
MESH = pl.DeviceIdType.MESH
K, V, Q, G = range(4)
O, DQ, DK, DV = range(4)
FIRST = 3


def dot_nt(a, b):
    return lax.dot_general(a, b, (((1,), (1,)), ((), ())), preferred_element_type=F32)


def dot_tn(a, b):
    return lax.dot_general(a, b, (((0,), (0,)), ((), ())), preferred_element_type=F32)


def layer(
    n_ctx, n_head, rows, all_rows,
    q_hbm, k_hbm, v_hbm, g_hbm, kdir_hbm, vdir_hbm, rew_hbm, end_hbm,
    o_hbm, dq_hbm, dk_hbm, dv_hbm,
    kdir_ref, vdir_ref, rew_ref, end_ref, got, sent, kbuf, vbuf, dk_acc, dv_acc, grad_send, grad_recv, small, suffix, ctx_val, ctx_got,
    vec_sem, own_sem, in_ssem, in_rsem, out_ssem, out_rsem,
    halo_ssem, halo_rsem, small_ssem, small_rsem, ctx_ssem, ctx_rsem,
):
    c = lax.axis_index("ctx")
    h = lax.axis_index("head")
    half = n_head // 2
    span = (half + 1) * rows
    score_scale = HEAD_DIM ** (-0.5)
    exp_scale = score_scale * math.log2(math.e)
    ins = (k_hbm, v_hbm, q_hbm, g_hbm)
    outs = (o_hbm, dq_hbm, dk_hbm, dv_hbm)
    around = [half] + [(d, n_head - d)[way] for d in reversed(range(1, half)) for way in range(2)]

    def head_at(off):
        return lax.rem(h + off, n_head)

    def at_ctx(off):
        return (lax.rem(c + off + n_ctx, n_ctx), h)

    def columns(off):
        return pl.ds(pl.multiple_of(head_at(off) * HEAD_DIM, HEAD_DIM), HEAD_DIM)

    def own_in(a):
        return pltpu.make_async_copy(ins[a].at[:, columns(0)], got.at[a, 0], own_sem.at[0, a])

    def own_out(a):
        return pltpu.make_async_copy(sent.at[a, 0], outs[a].at[:, columns(0)], own_sem.at[1, a])

    def send_in(a, j):
        return pltpu.make_async_remote_copy(
            src_ref=ins[a].at[:, columns(j)], dst_ref=got.at[a, n_head - j],
            send_sem=in_ssem.at[a, j], recv_sem=in_rsem.at[a, n_head - j],
            device_id=(c, head_at(j)), device_id_type=MESH,
        )

    def receive_in(a, j):
        return pltpu.make_async_remote_copy(
            src_ref=ins[a].at[:, columns(j)], dst_ref=got.at[a, j],
            send_sem=in_ssem.at[a, j], recv_sem=in_rsem.at[a, j],
            device_id=(c, head_at(j)), device_id_type=MESH,
        )

    def send_out(a, j):
        return pltpu.make_async_remote_copy(
            src_ref=sent.at[a, j], dst_ref=outs[a].at[:, columns(0)],
            send_sem=out_ssem.at[a, j], recv_sem=out_rsem.at[a, n_head - j],
            device_id=(c, head_at(j)), device_id_type=MESH,
        )

    def receive_out(a, j):
        return pltpu.make_async_remote_copy(
            src_ref=sent.at[a, j], dst_ref=outs[a].at[:, columns(j)],
            send_sem=out_ssem.at[a, j], recv_sem=out_rsem.at[a, j],
            device_id=(c, head_at(j)), device_id_type=MESH,
        )

    barrier = pltpu.get_barrier_semaphore()
    ctx_steps = [1 << k for k in range(n_ctx.bit_length() - 1)]
    senders = [(c, head_at(j)) for j in around] + [at_ctx(d) for d in [-1] + ctx_steps]
    for device in senders:
        pl.semaphore_signal(barrier, inc=1, device_id=device, device_id_type=MESH)
    vectors = [
        pltpu.make_async_copy(src, dst, vec_sem.at[i])
        for i, (src, dst) in enumerate(
            ((rew_hbm, rew_ref), (end_hbm, end_ref), (kdir_hbm, kdir_ref), (vdir_hbm, vdir_ref))
        )
    ]
    for copy in vectors:
        copy.start()
    pl.semaphore_wait(barrier, len(senders))
    for j in around[:FIRST]:
        send_in(K, j).start()
        send_in(V, j).start()

    vectors[0].wait()
    vectors[1].wait()
    lane = lax.broadcasted_iota(jnp.int32, (8, rows), 1)
    row = lax.broadcasted_iota(jnp.int32, (8, rows), 0)
    keep = jnp.broadcast_to((1 - end_ref[...]).astype(F32) * F32(1.0 - 1.0 / all_rows), (8, rows))
    total = jnp.broadcast_to(rew_ref[...].astype(F32) * 0.001, (8, rows))
    for k in range(rows.bit_length() - 1):
        d = 1 << k
        inside = lane < rows - d
        later_keep = jnp.where(inside, pltpu.roll(keep, rows - d, 1), 1.0)
        later_total = jnp.where(inside, pltpu.roll(total, rows - d, 1), 0.0)
        total = total + keep * later_total
        keep = keep * later_keep
    small[0] = jnp.where(row == 0, total, keep)
    def send_small(j):
        return pltpu.make_async_remote_copy(
            src_ref=small.at[0], dst_ref=small.at[n_head - j],
            send_sem=small_ssem.at[j], recv_sem=small_rsem.at[n_head - j],
            device_id=(c, head_at(j)), device_id_type=MESH,
        )

    def receive_small(j):
        return pltpu.make_async_remote_copy(
            src_ref=small.at[0], dst_ref=small.at[j],
            send_sem=small_ssem.at[j], recv_sem=small_rsem.at[j],
            device_id=(c, head_at(j)), device_id_type=MESH,
        )

    for j in around:
        send_small(j).start()
    for j in around[FIRST:]:
        send_in(K, j).start()
        send_in(V, j).start()
    for a in range(4):
        own_in(a).start()
    dk_acc[...] = jnp.zeros_like(dk_acc)
    dv_acc[...] = jnp.zeros_like(dv_acc)

    ctx_moves = [1] + ctx_steps

    def ctx_copy(k):
        return pltpu.make_async_remote_copy(
            src_ref=ctx_val.at[k], dst_ref=ctx_got.at[k],
            send_sem=ctx_ssem.at[k], recv_sem=ctx_rsem.at[k],
            device_id=at_ctx(-ctx_moves[k]), device_id_type=MESH,
        )

    def splat(ref, index, which):
        return jnp.broadcast_to(ref[index, which : which + 1, 0:1], (1, rows))

    def pair(total_row, keep_row):
        return jnp.where(row == 0, total_row, keep_row)

    for j in around:
        receive_small(j).wait_recv()
    after_total, after_keep = jnp.zeros((1, rows), F32), jnp.ones((1, rows), F32)
    for z in reversed(range(n_head)):
        suffix[z] = pair(after_total, after_keep)
        slot = lax.rem(z - h + n_head, n_head)
        z_total, z_keep = splat(small, slot, 0), splat(small, slot, 1)
        after_total = z_total + z_keep * after_total
        after_keep = z_keep * after_keep
    ctx_val[0] = pair(after_total, after_keep)
    ctx_copy(0).start()
    for k, d in enumerate(ctx_moves):
        ctx_copy(k).wait_recv()
        theirs, mine = ctx_got[k], ctx_val[k]
        ahead = c + d + (0 if k == 0 else 1)
        valid = jnp.broadcast_to(ahead, (8, rows)) < n_ctx
        got_total = jnp.where(valid, jnp.broadcast_to(theirs[0:1], (8, rows)), 0.0)
        got_keep = jnp.where(valid, jnp.broadcast_to(theirs[1:2], (8, rows)), 1.0)
        if k > 0:
            my_total = jnp.broadcast_to(mine[0:1], (8, rows))
            my_keep = jnp.broadcast_to(mine[1:2], (8, rows))
            got_total, got_keep = my_total + my_keep * got_total, my_keep * got_keep
        ctx_val[k + 1] = jnp.where(row == 0, got_total, got_keep)
        if k + 1 < len(ctx_moves):
            ctx_copy(k + 1).start()

    def finish(j):
        z = head_at(j)
        carry = ctx_val[len(ctx_moves), 0:1]
        carry_z = suffix[z, 0:1] + suffix[z, 1:2] * carry
        to_go = small[j, 0:1] + small[j, 1:2] * carry_z
        lifted = to_go * (4 * rows * n_head) ** (-0.5)
        column = jnp.broadcast_to(lifted, (rows, rows)).T
        place = pl.ds(pl.multiple_of((half + z) * rows, rows), rows)
        kbuf[place, :] = (got[K, j].astype(F32) + column * kdir_ref[pl.ds(h, 1), :]).astype(BF16)
        vbuf[place, :] = (got[V, j].astype(F32) + column * vdir_ref[pl.ds(h, 1), :]).astype(BF16)

    vectors[2].wait()
    vectors[3].wait()
    own_in(K).wait()
    own_in(V).wait()
    finish(0)
    for j in around:
        receive_in(K, j).wait_recv()
        receive_in(V, j).wait_recv()
        send_in(Q, j).start()
        send_in(G, j).start()
        finish(j)

    def halo(which):
        buf = (kbuf, vbuf)[which]
        return pltpu.make_async_remote_copy(
            src_ref=buf.at[pl.ds(n_head * rows, half * rows)], dst_ref=buf.at[pl.ds(0, half * rows)],
            send_sem=halo_ssem.at[which], recv_sem=halo_rsem.at[which],
            device_id=at_ctx(1), device_id_type=MESH,
        )

    halo(0).start()
    halo(1).start()
    own_in(Q).wait()
    own_in(G).wait()
    halo(0).wait_recv()
    halo(1).wait_recv()

    def slot_of(it):
        far = half - (it + 1) // 2
        odd = lax.rem(it, 2)
        return odd * far + (1 - odd) * (n_head - far)

    def tile(it, carry):
        j = slot_of(it)

        @pl.when(it < n_head - 1)
        def _():
            receive_in(Q, j).wait_recv()
            receive_in(G, j).wait_recv()

        t = head_at(j)
        place = pl.ds(pl.multiple_of(t * rows, rows), span)
        q, g, k, v = got[Q, j], got[G, j], kbuf[place, :], vbuf[place, :]
        key = lax.broadcasted_iota(jnp.int32, (span, rows), 0)
        query = lax.broadcasted_iota(jnp.int32, (span, rows), 1)
        before = jnp.where(c == 0, half * rows - t * rows, 0)
        allowed = (key >= jnp.maximum(query + 1, before)) & (key <= query + half * rows)
        s = jnp.where(allowed, dot_nt(k, q), -1e30)
        top = jnp.max(s, axis=0, keepdims=True)
        e = jnp.exp2((s - top) * exp_scale)
        probs = e * (1.0 / jnp.sum(e, axis=0, keepdims=True))
        weights = probs.astype(BF16)
        attended = dot_tn(weights, v).astype(BF16)
        row_dot = jnp.sum((attended.astype(F32) * g.astype(F32)).T, axis=0, keepdims=True)
        slopes = (probs * (dot_nt(v, g) - row_dot) * score_scale).astype(BF16)
        sent[O, j] = attended
        sent[DQ, j] = dot_tn(slopes, k).astype(BF16)

        @pl.when(it < n_head - 1)
        def _():
            send_out(O, j).start()
            send_out(DQ, j).start()

        dk_acc[place, :] += jnp.dot(slopes, q, preferred_element_type=F32)
        dv_acc[place, :] += jnp.dot(weights, g, preferred_element_type=F32)
        return carry

    lax.fori_loop(0, n_head, tile, 0)

    grad_send[0] = dk_acc[pl.ds(0, half * rows), :].astype(BF16)
    grad_send[1] = dv_acc[pl.ds(0, half * rows), :].astype(BF16)

    def grad(which):
        return pltpu.make_async_remote_copy(
            src_ref=grad_send.at[which], dst_ref=grad_recv.at[which],
            send_sem=halo_ssem.at[2 + which], recv_sem=halo_rsem.at[2 + which],
            device_id=at_ctx(-1), device_id_type=MESH,
        )

    grad(0).start()
    grad(1).start()
    own_out(O).start()
    own_out(DQ).start()
    grad(0).wait_recv()
    grad(1).wait_recv()

    def collect(it, carry):
        j = slot_of(it)
        z = head_at(j)
        place = pl.ds(pl.multiple_of((half + z) * rows, rows), rows)
        back = pl.ds(pl.multiple_of(jnp.maximum(z - half, 0) * rows, rows), rows)
        for which, acc in enumerate((dk_acc, dv_acc)):
            returned = jnp.where(z >= half, grad_recv[which, back, :].astype(F32), 0.0)
            sent[DK + which, j] = (acc[place, :] + returned).astype(BF16)

        @pl.when(it < n_head - 1)
        def _():
            send_out(DK, j).start()
            send_out(DV, j).start()

        return carry

    lax.fori_loop(0, n_head, collect, 0)
    own_out(DK).start()
    own_out(DV).start()

    for j in around:
        send_small(j).wait_send()
    for k in range(len(ctx_moves)):
        ctx_copy(k).wait_send()
    for which in range(2):
        halo(which).wait_send()
        grad(which).wait_send()
    for a in range(4):
        own_out(a).wait()
        for j in around:
            send_in(a, j).wait_send()
            send_out(a, j).wait_send()
            receive_out(a, j).wait_recv()


def on_device(queries, keys_base, values_base, grad_out, key_dir, value_dir, rewards, episode_end):
    rows, features = queries.shape
    n_ctx, n_head = lax.axis_size("ctx"), lax.axis_size("head")
    half = n_head // 2
    all_rows = rows * n_ctx * n_head
    unit = (rows, HEAD_DIM)
    ctx_moves = n_ctx.bit_length()
    hbm = pl.BlockSpec(memory_space=pl.ANY)
    dma = pltpu.SemaphoreType.DMA
    return pl.pallas_call(
        functools.partial(layer, n_ctx, n_head, rows, all_rows),
        out_shape=[jax.ShapeDtypeStruct((rows, features), BF16)] * 4,
        in_specs=[hbm] * 8,
        out_specs=[hbm] * 4,
        scratch_shapes=[
            pltpu.VMEM((n_head, HEAD_DIM), F32),
            pltpu.VMEM((n_head, HEAD_DIM), F32),
            pltpu.VMEM((1, rows), jnp.int32),
            pltpu.VMEM((1, rows), jnp.int32),
            pltpu.VMEM((4, n_head) + unit, BF16),
            pltpu.VMEM((4, n_head) + unit, BF16),
            pltpu.VMEM(((n_head + half) * rows, HEAD_DIM), BF16),
            pltpu.VMEM(((n_head + half) * rows, HEAD_DIM), BF16),
            pltpu.VMEM(((n_head + half) * rows, HEAD_DIM), F32),
            pltpu.VMEM(((n_head + half) * rows, HEAD_DIM), F32),
            pltpu.VMEM((2, half * rows, HEAD_DIM), BF16),
            pltpu.VMEM((2, half * rows, HEAD_DIM), BF16),
            pltpu.VMEM((n_head, 8, rows), F32),
            pltpu.VMEM((n_head, 8, rows), F32),
            pltpu.VMEM((ctx_moves + 1, 8, rows), F32),
            pltpu.VMEM((ctx_moves, 8, rows), F32),
            dma((4,)),
            dma((2, 4)),
            dma((4, n_head)),
            dma((4, n_head)),
            dma((4, n_head)),
            dma((4, n_head)),
            dma((4,)),
            dma((4,)),
            dma((n_head,)),
            dma((n_head,)),
            dma((ctx_moves,)),
            dma((ctx_moves,)),
        ],
        compiler_params=pltpu.CompilerParams(
            collective_id=0, has_side_effects=True, vmem_limit_bytes=60 * 2**20
        ),
    )(
        queries, keys_base, values_base, grad_out,
        key_dir.reshape(n_head, HEAD_DIM), value_dir.reshape(n_head, HEAD_DIM),
        rewards.reshape(1, rows), episode_end.reshape(1, rows),
    )


def solution(mesh):
    wide = P(("ctx", "head"), None)
    steps = P(("ctx", "head"))
    return jax.shard_map(
        on_device,
        mesh=mesh,
        in_specs=(wide, wide, wide, wide, P(), P(), steps, steps),
        out_specs=(wide, wide, wide, wide),
        check_vma=False,
    )
```

```python
import functools
import math

import jax
import jax.numpy as jnp
from jax import lax
from jax.experimental import pallas as pl
from jax.experimental.pallas import tpu as pltpu
from jax.sharding import PartitionSpec as P

HEAD_DIM = 128
BF16 = jnp.bfloat16
F32 = jnp.float32
MESH = pl.DeviceIdType.MESH
K, V, Q, G = range(4)
O, DQ, DK, DV = range(4)
FIRST = 3
PIECES = 2


def dot_nt(a, b):
    return lax.dot_general(a, b, (((1,), (1,)), ((), ())), preferred_element_type=F32)


def dot_tn(a, b):
    return lax.dot_general(a, b, (((0,), (0,)), ((), ())), preferred_element_type=F32)


def layer(
    n_ctx, n_head, rows, all_rows,
    q_hbm, k_hbm, v_hbm, g_hbm, kdir_hbm, vdir_hbm, rew_hbm, end_hbm,
    o_hbm, dq_hbm, dk_hbm, dv_hbm,
    kdir_ref, vdir_ref, rew_ref, end_ref, got, sent, kbuf, vbuf, dk_acc, dv_acc, grad_send, grad_recv, small, suffix, ctx_val, ctx_got,
    vec_sem, own_sem, in_ssem, in_rsem, out_ssem, out_rsem,
    halo_ssem, halo_rsem, small_ssem, small_rsem, ctx_ssem, ctx_rsem,
):
    c = lax.axis_index("ctx")
    h = lax.axis_index("head")
    half = n_head // 2
    span = (half + 1) * rows
    score_scale = HEAD_DIM ** (-0.5)
    exp_scale = score_scale * math.log2(math.e)
    ins = (k_hbm, v_hbm, q_hbm, g_hbm)
    outs = (o_hbm, dq_hbm, dk_hbm, dv_hbm)
    around = [half] + [(d, n_head - d)[way] for d in reversed(range(1, half)) for way in range(2)]

    def head_at(off):
        return lax.rem(h + off, n_head)

    def at_ctx(off):
        return (lax.rem(c + off + n_ctx, n_ctx), h)

    def columns(off):
        return pl.ds(pl.multiple_of(head_at(off) * HEAD_DIM, HEAD_DIM), HEAD_DIM)

    def own_in(a):
        return pltpu.make_async_copy(ins[a].at[:, columns(0)], got.at[a, 0], own_sem.at[0, a])

    def own_out(a):
        return pltpu.make_async_copy(sent.at[a, 0], outs[a].at[:, columns(0)], own_sem.at[1, a])

    def send_in(a, j):
        return pltpu.make_async_remote_copy(
            src_ref=ins[a].at[:, columns(j)], dst_ref=got.at[a, n_head - j],
            send_sem=in_ssem.at[a, j], recv_sem=in_rsem.at[a, n_head - j],
            device_id=(c, head_at(j)), device_id_type=MESH,
        )

    def receive_in(a, j):
        return pltpu.make_async_remote_copy(
            src_ref=ins[a].at[:, columns(j)], dst_ref=got.at[a, j],
            send_sem=in_ssem.at[a, j], recv_sem=in_rsem.at[a, j],
            device_id=(c, head_at(j)), device_id_type=MESH,
        )

    def send_out(a, j):
        return pltpu.make_async_remote_copy(
            src_ref=sent.at[a, j], dst_ref=outs[a].at[:, columns(0)],
            send_sem=out_ssem.at[a, j], recv_sem=out_rsem.at[a, n_head - j],
            device_id=(c, head_at(j)), device_id_type=MESH,
        )

    def receive_out(a, j):
        return pltpu.make_async_remote_copy(
            src_ref=sent.at[a, j], dst_ref=outs[a].at[:, columns(j)],
            send_sem=out_ssem.at[a, j], recv_sem=out_rsem.at[a, j],
            device_id=(c, head_at(j)), device_id_type=MESH,
        )

    barrier = pltpu.get_barrier_semaphore()
    ctx_steps = [1 << k for k in range(n_ctx.bit_length() - 1)]
    senders = [(c, head_at(j)) for j in around] + [at_ctx(d) for d in [-1] + ctx_steps]
    for device in senders:
        pl.semaphore_signal(barrier, inc=1, device_id=device, device_id_type=MESH)
    vectors = [
        pltpu.make_async_copy(src, dst, vec_sem.at[i])
        for i, (src, dst) in enumerate(
            ((rew_hbm, rew_ref), (end_hbm, end_ref), (kdir_hbm, kdir_ref), (vdir_hbm, vdir_ref))
        )
    ]
    for copy in vectors:
        copy.start()
    pl.semaphore_wait(barrier, len(senders))
    for j in around[:FIRST]:
        send_in(K, j).start()
        send_in(V, j).start()

    vectors[0].wait()
    vectors[1].wait()
    lane = lax.broadcasted_iota(jnp.int32, (8, rows), 1)
    row = lax.broadcasted_iota(jnp.int32, (8, rows), 0)
    keep = jnp.broadcast_to((1 - end_ref[...]).astype(F32) * F32(1.0 - 1.0 / all_rows), (8, rows))
    total = jnp.broadcast_to(rew_ref[...].astype(F32) * 0.001, (8, rows))
    for k in range(rows.bit_length() - 1):
        d = 1 << k
        inside = lane < rows - d
        later_keep = jnp.where(inside, pltpu.roll(keep, rows - d, 1), 1.0)
        later_total = jnp.where(inside, pltpu.roll(total, rows - d, 1), 0.0)
        total = total + keep * later_total
        keep = keep * later_keep
    small[0] = jnp.where(row == 0, total, keep)
    def send_small(j):
        return pltpu.make_async_remote_copy(
            src_ref=small.at[0], dst_ref=small.at[n_head - j],
            send_sem=small_ssem.at[j], recv_sem=small_rsem.at[n_head - j],
            device_id=(c, head_at(j)), device_id_type=MESH,
        )

    def receive_small(j):
        return pltpu.make_async_remote_copy(
            src_ref=small.at[0], dst_ref=small.at[j],
            send_sem=small_ssem.at[j], recv_sem=small_rsem.at[j],
            device_id=(c, head_at(j)), device_id_type=MESH,
        )

    for j in around:
        send_small(j).start()
    for j in around[FIRST:]:
        send_in(K, j).start()
        send_in(V, j).start()
    for a in range(4):
        own_in(a).start()
    dk_acc[...] = jnp.zeros_like(dk_acc)
    dv_acc[...] = jnp.zeros_like(dv_acc)

    ctx_moves = [1] + ctx_steps

    def ctx_copy(k):
        return pltpu.make_async_remote_copy(
            src_ref=ctx_val.at[k], dst_ref=ctx_got.at[k],
            send_sem=ctx_ssem.at[k], recv_sem=ctx_rsem.at[k],
            device_id=at_ctx(-ctx_moves[k]), device_id_type=MESH,
        )

    def splat(ref, index, which):
        return jnp.broadcast_to(ref[index, which : which + 1, 0:1], (1, rows))

    def pair(total_row, keep_row):
        return jnp.where(row == 0, total_row, keep_row)

    for j in around:
        receive_small(j).wait_recv()
    after_total, after_keep = jnp.zeros((1, rows), F32), jnp.ones((1, rows), F32)
    for z in reversed(range(n_head)):
        suffix[z] = pair(after_total, after_keep)
        slot = lax.rem(z - h + n_head, n_head)
        z_total, z_keep = splat(small, slot, 0), splat(small, slot, 1)
        after_total = z_total + z_keep * after_total
        after_keep = z_keep * after_keep
    ctx_val[0] = pair(after_total, after_keep)
    ctx_copy(0).start()
    for k, d in enumerate(ctx_moves):
        ctx_copy(k).wait_recv()
        theirs, mine = ctx_got[k], ctx_val[k]
        ahead = c + d + (0 if k == 0 else 1)
        valid = jnp.broadcast_to(ahead, (8, rows)) < n_ctx
        got_total = jnp.where(valid, jnp.broadcast_to(theirs[0:1], (8, rows)), 0.0)
        got_keep = jnp.where(valid, jnp.broadcast_to(theirs[1:2], (8, rows)), 1.0)
        if k > 0:
            my_total = jnp.broadcast_to(mine[0:1], (8, rows))
            my_keep = jnp.broadcast_to(mine[1:2], (8, rows))
            got_total, got_keep = my_total + my_keep * got_total, my_keep * got_keep
        ctx_val[k + 1] = jnp.where(row == 0, got_total, got_keep)
        if k + 1 < len(ctx_moves):
            ctx_copy(k + 1).start()

    def finish(j):
        z = head_at(j)
        carry = ctx_val[len(ctx_moves), 0:1]
        carry_z = suffix[z, 0:1] + suffix[z, 1:2] * carry
        to_go = small[j, 0:1] + small[j, 1:2] * carry_z
        lifted = to_go * (4 * rows * n_head) ** (-0.5)
        column = jnp.broadcast_to(lifted, (rows, rows)).T
        place = pl.ds(pl.multiple_of((half + z) * rows, rows), rows)
        kbuf[place, :] = (got[K, j].astype(F32) + column * kdir_ref[pl.ds(h, 1), :]).astype(BF16)
        vbuf[place, :] = (got[V, j].astype(F32) + column * vdir_ref[pl.ds(h, 1), :]).astype(BF16)

    vectors[2].wait()
    vectors[3].wait()
    own_in(K).wait()
    own_in(V).wait()
    finish(0)
    for j in around:
        receive_in(K, j).wait_recv()
        receive_in(V, j).wait_recv()
        send_in(Q, j).start()
        send_in(G, j).start()
        finish(j)

    def halo(which):
        buf = (kbuf, vbuf)[which]
        return pltpu.make_async_remote_copy(
            src_ref=buf.at[pl.ds(n_head * rows, half * rows)], dst_ref=buf.at[pl.ds(0, half * rows)],
            send_sem=halo_ssem.at[which], recv_sem=halo_rsem.at[which],
            device_id=at_ctx(1), device_id_type=MESH,
        )

    halo(0).start()
    halo(1).start()
    own_in(Q).wait()
    own_in(G).wait()
    halo(0).wait_recv()
    halo(1).wait_recv()

    def slot_of(it):
        far = half - (it + 1) // 2
        odd = lax.rem(it, 2)
        return odd * far + (1 - odd) * (n_head - far)

    def tile(it, carry):
        j = slot_of(it)

        @pl.when(it < n_head - 1)
        def _():
            receive_in(Q, j).wait_recv()
            receive_in(G, j).wait_recv()

        t = head_at(j)
        place = pl.ds(pl.multiple_of(t * rows, rows), span)
        q, g, k, v = got[Q, j], got[G, j], kbuf[place, :], vbuf[place, :]
        key = lax.broadcasted_iota(jnp.int32, (span, rows), 0)
        query = lax.broadcasted_iota(jnp.int32, (span, rows), 1)
        before = jnp.where(c == 0, half * rows - t * rows, 0)
        allowed = (key >= jnp.maximum(query + 1, before)) & (key <= query + half * rows)
        s = jnp.where(allowed, dot_nt(k, q), -1e30)
        top = jnp.max(s, axis=0, keepdims=True)
        e = jnp.exp2((s - top) * exp_scale)
        probs = e * (1.0 / jnp.sum(e, axis=0, keepdims=True))
        weights = probs.astype(BF16)
        attended = dot_tn(weights, v).astype(BF16)
        row_dot = jnp.sum((attended.astype(F32) * g.astype(F32)).T, axis=0, keepdims=True)
        slopes = (probs * (dot_nt(v, g) - row_dot) * score_scale).astype(BF16)
        sent[O, j] = attended
        sent[DQ, j] = dot_tn(slopes, k).astype(BF16)

        @pl.when(it < n_head - 1)
        def _():
            send_out(O, j).start()
            send_out(DQ, j).start()

        dk_acc[place, :] += jnp.dot(slopes, q, preferred_element_type=F32)
        dv_acc[place, :] += jnp.dot(weights, g, preferred_element_type=F32)
        return carry

    lax.fori_loop(0, n_head, tile, 0)

    grad_send[0] = dk_acc[pl.ds(0, half * rows), :].astype(BF16)
    grad_send[1] = dv_acc[pl.ds(0, half * rows), :].astype(BF16)

    def grad(which):
        return pltpu.make_async_remote_copy(
            src_ref=grad_send.at[which], dst_ref=grad_recv.at[which],
            send_sem=halo_ssem.at[2 + which], recv_sem=halo_rsem.at[2 + which],
            device_id=at_ctx(-1), device_id_type=MESH,
        )

    grad(0).start()
    grad(1).start()
    own_out(O).start()
    own_out(DQ).start()
    grad(0).wait_recv()
    grad(1).wait_recv()

    def collect(it, carry):
        j = slot_of(it)
        z = head_at(j)
        place = pl.ds(pl.multiple_of((half + z) * rows, rows), rows)
        back = pl.ds(pl.multiple_of(jnp.maximum(z - half, 0) * rows, rows), rows)
        for which, acc in enumerate((dk_acc, dv_acc)):
            returned = jnp.where(z >= half, grad_recv[which, back, :].astype(F32), 0.0)
            sent[DK + which, j] = (acc[place, :] + returned).astype(BF16)

        @pl.when(it < n_head - 1)
        def _():
            send_out(DK, j).start()
            send_out(DV, j).start()

        return carry

    lax.fori_loop(0, n_head, collect, 0)
    own_out(DK).start()
    own_out(DV).start()

    for j in around:
        send_small(j).wait_send()
    for k in range(len(ctx_moves)):
        ctx_copy(k).wait_send()
    for which in range(2):
        halo(which).wait_send()
        grad(which).wait_send()
    for a in range(4):
        own_out(a).wait()
        for j in around:
            send_in(a, j).wait_send()
            send_out(a, j).wait_send()
            receive_out(a, j).wait_recv()


def hand_over(*refs):
    held, in_sem, out_sem = refs[8:]
    rows = refs[0].shape[0] // PIECES
    pieces = [(a, i, pl.ds(i * rows, rows)) for a in range(4) for i in range(PIECES)]

    def inward(a, i, part):
        return pltpu.make_async_copy(refs[a].at[part], held.at[a, part], in_sem.at[a, i])

    def outward(a, i, part):
        return pltpu.make_async_copy(held.at[a, part], refs[4 + a].at[part], out_sem.at[a, i])

    for piece in pieces:
        inward(*piece).start()
    for piece in pieces:
        inward(*piece).wait()
        outward(*piece).start()
    for piece in pieces:
        outward(*piece).wait()


def on_device(queries, keys_base, values_base, grad_out, key_dir, value_dir, rewards, episode_end):
    rows, features = queries.shape
    n_ctx, n_head = lax.axis_size("ctx"), lax.axis_size("head")
    half = n_head // 2
    all_rows = rows * n_ctx * n_head
    unit = (rows, HEAD_DIM)
    ctx_moves = n_ctx.bit_length()
    hbm = pl.BlockSpec(memory_space=pl.ANY)
    dma = pltpu.SemaphoreType.DMA
    results = pl.pallas_call(
        functools.partial(layer, n_ctx, n_head, rows, all_rows),
        out_shape=[jax.ShapeDtypeStruct((rows, features), BF16)] * 4,
        in_specs=[hbm] * 8,
        out_specs=[hbm] * 4,
        scratch_shapes=[
            pltpu.VMEM((n_head, HEAD_DIM), F32),
            pltpu.VMEM((n_head, HEAD_DIM), F32),
            pltpu.VMEM((1, rows), jnp.int32),
            pltpu.VMEM((1, rows), jnp.int32),
            pltpu.VMEM((4, n_head) + unit, BF16),
            pltpu.VMEM((4, n_head) + unit, BF16),
            pltpu.VMEM(((n_head + half) * rows, HEAD_DIM), BF16),
            pltpu.VMEM(((n_head + half) * rows, HEAD_DIM), BF16),
            pltpu.VMEM(((n_head + half) * rows, HEAD_DIM), F32),
            pltpu.VMEM(((n_head + half) * rows, HEAD_DIM), F32),
            pltpu.VMEM((2, half * rows, HEAD_DIM), BF16),
            pltpu.VMEM((2, half * rows, HEAD_DIM), BF16),
            pltpu.VMEM((n_head, 8, rows), F32),
            pltpu.VMEM((n_head, 8, rows), F32),
            pltpu.VMEM((ctx_moves + 1, 8, rows), F32),
            pltpu.VMEM((ctx_moves, 8, rows), F32),
            dma((4,)),
            dma((2, 4)),
            dma((4, n_head)),
            dma((4, n_head)),
            dma((4, n_head)),
            dma((4, n_head)),
            dma((4,)),
            dma((4,)),
            dma((n_head,)),
            dma((n_head,)),
            dma((ctx_moves,)),
            dma((ctx_moves,)),
        ],
        compiler_params=pltpu.CompilerParams(
            collective_id=0, has_side_effects=True, vmem_limit_bytes=60 * 2**20
        ),
    )(
        queries, keys_base, values_base, grad_out,
        key_dir.reshape(n_head, HEAD_DIM), value_dir.reshape(n_head, HEAD_DIM),
        rewards.reshape(1, rows), episode_end.reshape(1, rows),
    )
    return pl.pallas_call(
        hand_over,
        out_shape=[jax.ShapeDtypeStruct((rows, features), BF16)] * 4,
        in_specs=[hbm] * 4,
        out_specs=[hbm] * 4,
        scratch_shapes=[pltpu.VMEM((4, rows, features), BF16), dma((4, PIECES)), dma((4, PIECES))],
        compiler_params=pltpu.CompilerParams(vmem_limit_bytes=60 * 2**20),
    )(*results)


def solution(mesh):
    wide = P(("ctx", "head"), None)
    steps = P(("ctx", "head"))
    return jax.shard_map(
        on_device,
        mesh=mesh,
        in_specs=(wide, wide, wide, wide, P(), P(), steps, steps),
        out_specs=(wide, wide, wide, wide),
        check_vma=False,
    )
```

```python
import functools
import math

import jax
import jax.numpy as jnp
from jax import lax
from jax.experimental import pallas as pl
from jax.experimental.pallas import tpu as pltpu
from jax.sharding import PartitionSpec as P

HEAD_DIM = 128
BF16 = jnp.bfloat16
F32 = jnp.float32
MESH = pl.DeviceIdType.MESH
K, V, Q, G = range(4)
O, DQ, DK, DV = range(4)
FIRST = 3
PIECES = 2


def dot_nt(a, b):
    return lax.dot_general(a, b, (((1,), (1,)), ((), ())), preferred_element_type=F32)


def dot_tn(a, b):
    return lax.dot_general(a, b, (((0,), (0,)), ((), ())), preferred_element_type=F32)


def layer(
    n_ctx, n_head, rows, all_rows,
    q_hbm, k_hbm, v_hbm, g_hbm, kdir_hbm, vdir_hbm, rew_hbm, end_hbm,
    o_hbm, dq_hbm, dk_hbm, dv_hbm,
    kdir_ref, vdir_ref, rew_ref, end_ref, got, sent, kbuf, vbuf, dk_acc, dv_acc, grad_send, grad_recv, small, suffix, ctx_val, ctx_got,
    vec_sem, own_sem, in_ssem, in_rsem, out_ssem, out_rsem,
    halo_ssem, halo_rsem, small_ssem, small_rsem, ctx_ssem, ctx_rsem,
):
    c = lax.axis_index("ctx")
    h = lax.axis_index("head")
    half = n_head // 2
    span = (half + 1) * rows
    score_scale = HEAD_DIM ** (-0.5)
    exp_scale = score_scale * math.log2(math.e)
    ins = (k_hbm, v_hbm, q_hbm, g_hbm)
    outs = (o_hbm, dq_hbm, dk_hbm, dv_hbm)
    around = [half] + [(d, n_head - d)[way] for d in reversed(range(1, half)) for way in range(2)]

    def head_at(off):
        return lax.rem(h + off, n_head)

    def at_ctx(off):
        return (lax.rem(c + off + n_ctx, n_ctx), h)

    def columns(off):
        return pl.ds(pl.multiple_of(head_at(off) * HEAD_DIM, HEAD_DIM), HEAD_DIM)

    def own_in(a):
        return pltpu.make_async_copy(ins[a].at[:, columns(0)], got.at[a, 0], own_sem.at[0, a])

    def own_out(a):
        return pltpu.make_async_copy(sent.at[a, 0], outs[a].at[:, columns(0)], own_sem.at[1, a])

    def send_in(a, j):
        return pltpu.make_async_remote_copy(
            src_ref=ins[a].at[:, columns(j)], dst_ref=got.at[a, n_head - j],
            send_sem=in_ssem.at[a, j], recv_sem=in_rsem.at[a, n_head - j],
            device_id=(c, head_at(j)), device_id_type=MESH,
        )

    def receive_in(a, j):
        return pltpu.make_async_remote_copy(
            src_ref=ins[a].at[:, columns(j)], dst_ref=got.at[a, j],
            send_sem=in_ssem.at[a, j], recv_sem=in_rsem.at[a, j],
            device_id=(c, head_at(j)), device_id_type=MESH,
        )

    def send_out(a, j):
        return pltpu.make_async_remote_copy(
            src_ref=sent.at[a, j], dst_ref=outs[a].at[:, columns(0)],
            send_sem=out_ssem.at[a, j], recv_sem=out_rsem.at[a, n_head - j],
            device_id=(c, head_at(j)), device_id_type=MESH,
        )

    def receive_out(a, j):
        return pltpu.make_async_remote_copy(
            src_ref=sent.at[a, j], dst_ref=outs[a].at[:, columns(j)],
            send_sem=out_ssem.at[a, j], recv_sem=out_rsem.at[a, j],
            device_id=(c, head_at(j)), device_id_type=MESH,
        )

    barrier = pltpu.get_barrier_semaphore()
    ctx_steps = [1 << k for k in range(n_ctx.bit_length() - 1)]
    senders = [(c, head_at(j)) for j in around] + [at_ctx(d) for d in [-1] + ctx_steps]
    for device in senders:
        pl.semaphore_signal(barrier, inc=1, device_id=device, device_id_type=MESH)
    vectors = [
        pltpu.make_async_copy(src, dst, vec_sem.at[i])
        for i, (src, dst) in enumerate(
            ((rew_hbm, rew_ref), (end_hbm, end_ref), (kdir_hbm, kdir_ref), (vdir_hbm, vdir_ref))
        )
    ]
    for copy in vectors:
        copy.start()
    pl.semaphore_wait(barrier, len(senders))
    for j in around[:FIRST]:
        send_in(K, j).start()
        send_in(V, j).start()

    vectors[0].wait()
    vectors[1].wait()
    lane = lax.broadcasted_iota(jnp.int32, (8, rows), 1)
    row = lax.broadcasted_iota(jnp.int32, (8, rows), 0)
    keep = jnp.broadcast_to((1 - end_ref[...]).astype(F32) * F32(1.0 - 1.0 / all_rows), (8, rows))
    total = jnp.broadcast_to(rew_ref[...].astype(F32) * 0.001, (8, rows))
    for k in range(rows.bit_length() - 1):
        d = 1 << k
        inside = lane < rows - d
        later_keep = jnp.where(inside, pltpu.roll(keep, rows - d, 1), 1.0)
        later_total = jnp.where(inside, pltpu.roll(total, rows - d, 1), 0.0)
        total = total + keep * later_total
        keep = keep * later_keep
    small[0] = jnp.where(row == 0, total, keep)[0:2]
    def send_small(j):
        return pltpu.make_async_remote_copy(
            src_ref=small.at[0], dst_ref=small.at[n_head - j],
            send_sem=small_ssem.at[j], recv_sem=small_rsem.at[n_head - j],
            device_id=(c, head_at(j)), device_id_type=MESH,
        )

    def receive_small(j):
        return pltpu.make_async_remote_copy(
            src_ref=small.at[0], dst_ref=small.at[j],
            send_sem=small_ssem.at[j], recv_sem=small_rsem.at[j],
            device_id=(c, head_at(j)), device_id_type=MESH,
        )

    for j in around:
        send_small(j).start()
    for j in around[FIRST:]:
        send_in(K, j).start()
        send_in(V, j).start()
    for a in range(4):
        own_in(a).start()
    dk_acc[...] = jnp.zeros_like(dk_acc)
    dv_acc[...] = jnp.zeros_like(dv_acc)

    ctx_moves = [1] + ctx_steps

    def ctx_copy(k):
        return pltpu.make_async_remote_copy(
            src_ref=ctx_val.at[k], dst_ref=ctx_got.at[k],
            send_sem=ctx_ssem.at[k], recv_sem=ctx_rsem.at[k],
            device_id=at_ctx(-ctx_moves[k]), device_id_type=MESH,
        )

    def splat(ref, index, which):
        return jnp.broadcast_to(ref[index, which : which + 1, 0:1], (1, rows))

    def pair(total_row, keep_row):
        return jnp.where(row == 0, total_row, keep_row)

    for j in around:
        receive_small(j).wait_recv()
    after_total, after_keep = jnp.zeros((1, rows), F32), jnp.ones((1, rows), F32)
    for z in reversed(range(n_head)):
        suffix[z] = pair(after_total, after_keep)
        slot = lax.rem(z - h + n_head, n_head)
        z_total, z_keep = splat(small, slot, 0), splat(small, slot, 1)
        after_total = z_total + z_keep * after_total
        after_keep = z_keep * after_keep
    ctx_val[0] = pair(after_total, after_keep)
    ctx_copy(0).start()
    for k, d in enumerate(ctx_moves):
        ctx_copy(k).wait_recv()
        theirs, mine = ctx_got[k], ctx_val[k]
        ahead = c + d + (0 if k == 0 else 1)
        valid = jnp.broadcast_to(ahead, (8, rows)) < n_ctx
        got_total = jnp.where(valid, jnp.broadcast_to(theirs[0:1], (8, rows)), 0.0)
        got_keep = jnp.where(valid, jnp.broadcast_to(theirs[1:2], (8, rows)), 1.0)
        if k > 0:
            my_total = jnp.broadcast_to(mine[0:1], (8, rows))
            my_keep = jnp.broadcast_to(mine[1:2], (8, rows))
            got_total, got_keep = my_total + my_keep * got_total, my_keep * got_keep
        ctx_val[k + 1] = jnp.where(row == 0, got_total, got_keep)
        if k + 1 < len(ctx_moves):
            ctx_copy(k + 1).start()

    def finish(j):
        z = head_at(j)
        carry = ctx_val[len(ctx_moves), 0:1]
        carry_z = suffix[z, 0:1] + suffix[z, 1:2] * carry
        to_go = small[j, 0:1] + small[j, 1:2] * carry_z
        lifted = to_go * (4 * rows * n_head) ** (-0.5)
        column = jnp.broadcast_to(lifted, (rows, rows)).T
        place = pl.ds(pl.multiple_of((half + z) * rows, rows), rows)
        kbuf[place, :] = (got[K, j].astype(F32) + column * kdir_ref[pl.ds(h, 1), :]).astype(BF16)
        vbuf[place, :] = (got[V, j].astype(F32) + column * vdir_ref[pl.ds(h, 1), :]).astype(BF16)

    vectors[2].wait()
    vectors[3].wait()
    own_in(K).wait()
    own_in(V).wait()
    finish(0)
    for j in around:
        receive_in(K, j).wait_recv()
        receive_in(V, j).wait_recv()
        send_in(Q, j).start()
        send_in(G, j).start()
        finish(j)

    def halo(which):
        buf = (kbuf, vbuf)[which]
        return pltpu.make_async_remote_copy(
            src_ref=buf.at[pl.ds(n_head * rows, half * rows)], dst_ref=buf.at[pl.ds(0, half * rows)],
            send_sem=halo_ssem.at[which], recv_sem=halo_rsem.at[which],
            device_id=at_ctx(1), device_id_type=MESH,
        )

    halo(0).start()
    halo(1).start()
    own_in(Q).wait()
    own_in(G).wait()
    halo(0).wait_recv()
    halo(1).wait_recv()

    def slot_of(it):
        far = half - (it + 1) // 2
        odd = lax.rem(it, 2)
        return odd * far + (1 - odd) * (n_head - far)

    def tile(it, carry):
        j = slot_of(it)

        @pl.when(it < n_head - 1)
        def _():
            receive_in(Q, j).wait_recv()
            receive_in(G, j).wait_recv()

        t = head_at(j)
        place = pl.ds(pl.multiple_of(t * rows, rows), span)
        q, g, k, v = got[Q, j], got[G, j], kbuf[place, :], vbuf[place, :]
        key = lax.broadcasted_iota(jnp.int32, (span, rows), 0)
        query = lax.broadcasted_iota(jnp.int32, (span, rows), 1)
        before = jnp.where(c == 0, half * rows - t * rows, 0)
        allowed = (key >= jnp.maximum(query + 1, before)) & (key <= query + half * rows)
        s = jnp.where(allowed, dot_nt(k, q), -1e30)
        top = jnp.max(s, axis=0, keepdims=True)
        e = jnp.exp2((s - top) * exp_scale)
        probs = e * (1.0 / jnp.sum(e, axis=0, keepdims=True))
        weights = probs.astype(BF16)
        attended = dot_tn(weights, v).astype(BF16)
        row_dot = jnp.sum((attended.astype(F32) * g.astype(F32)).T, axis=0, keepdims=True)
        slopes = (probs * (dot_nt(v, g) - row_dot) * score_scale).astype(BF16)
        sent[O, j] = attended
        sent[DQ, j] = dot_tn(slopes, k).astype(BF16)

        @pl.when(it < n_head - 1)
        def _():
            send_out(O, j).start()
            send_out(DQ, j).start()

        dk_acc[place, :] += jnp.dot(slopes, q, preferred_element_type=F32)
        dv_acc[place, :] += jnp.dot(weights, g, preferred_element_type=F32)
        return carry

    lax.fori_loop(0, n_head, tile, 0)

    grad_send[0] = dk_acc[pl.ds(0, half * rows), :].astype(BF16)
    grad_send[1] = dv_acc[pl.ds(0, half * rows), :].astype(BF16)

    def grad(which):
        return pltpu.make_async_remote_copy(
            src_ref=grad_send.at[which], dst_ref=grad_recv.at[which],
            send_sem=halo_ssem.at[2 + which], recv_sem=halo_rsem.at[2 + which],
            device_id=at_ctx(-1), device_id_type=MESH,
        )

    grad(0).start()
    grad(1).start()
    own_out(O).start()
    own_out(DQ).start()
    grad(0).wait_recv()
    grad(1).wait_recv()

    def collect(it, carry):
        j = slot_of(it)
        z = head_at(j)
        place = pl.ds(pl.multiple_of((half + z) * rows, rows), rows)
        back = pl.ds(pl.multiple_of(jnp.maximum(z - half, 0) * rows, rows), rows)
        for which, acc in enumerate((dk_acc, dv_acc)):
            returned = jnp.where(z >= half, grad_recv[which, back, :].astype(F32), 0.0)
            sent[DK + which, j] = (acc[place, :] + returned).astype(BF16)

        @pl.when(it < n_head - 1)
        def _():
            send_out(DK, j).start()
            send_out(DV, j).start()

        return carry

    lax.fori_loop(0, n_head, collect, 0)
    own_out(DK).start()
    own_out(DV).start()

    for j in around:
        send_small(j).wait_send()
    for k in range(len(ctx_moves)):
        ctx_copy(k).wait_send()
    for which in range(2):
        halo(which).wait_send()
        grad(which).wait_send()
    for a in range(4):
        own_out(a).wait()
        for j in around:
            send_in(a, j).wait_send()
            send_out(a, j).wait_send()
            receive_out(a, j).wait_recv()


def hand_over(*refs):
    held, in_sem, out_sem = refs[8:]
    rows = refs[0].shape[0] // PIECES
    pieces = [(a, i, pl.ds(i * rows, rows)) for a in range(4) for i in range(PIECES)]

    def inward(a, i, part):
        return pltpu.make_async_copy(refs[a].at[part], held.at[a, part], in_sem.at[a, i])

    def outward(a, i, part):
        return pltpu.make_async_copy(held.at[a, part], refs[4 + a].at[part], out_sem.at[a, i])

    for piece in pieces:
        inward(*piece).start()
    for piece in pieces:
        inward(*piece).wait()
        outward(*piece).start()
    for piece in pieces:
        outward(*piece).wait()


def on_device(queries, keys_base, values_base, grad_out, key_dir, value_dir, rewards, episode_end):
    rows, features = queries.shape
    n_ctx, n_head = lax.axis_size("ctx"), lax.axis_size("head")
    half = n_head // 2
    all_rows = rows * n_ctx * n_head
    unit = (rows, HEAD_DIM)
    ctx_moves = n_ctx.bit_length()
    hbm = pl.BlockSpec(memory_space=pl.ANY)
    dma = pltpu.SemaphoreType.DMA
    results = pl.pallas_call(
        functools.partial(layer, n_ctx, n_head, rows, all_rows),
        out_shape=[jax.ShapeDtypeStruct((rows, features), BF16)] * 4,
        in_specs=[hbm] * 8,
        out_specs=[hbm] * 4,
        scratch_shapes=[
            pltpu.VMEM((n_head, HEAD_DIM), F32),
            pltpu.VMEM((n_head, HEAD_DIM), F32),
            pltpu.VMEM((1, rows), jnp.int32),
            pltpu.VMEM((1, rows), jnp.int32),
            pltpu.VMEM((4, n_head) + unit, BF16),
            pltpu.VMEM((4, n_head) + unit, BF16),
            pltpu.VMEM(((n_head + half) * rows, HEAD_DIM), BF16),
            pltpu.VMEM(((n_head + half) * rows, HEAD_DIM), BF16),
            pltpu.VMEM(((n_head + half) * rows, HEAD_DIM), F32),
            pltpu.VMEM(((n_head + half) * rows, HEAD_DIM), F32),
            pltpu.VMEM((2, half * rows, HEAD_DIM), BF16),
            pltpu.VMEM((2, half * rows, HEAD_DIM), BF16),
            pltpu.VMEM((n_head, 2, rows), F32),
            pltpu.VMEM((n_head, 8, rows), F32),
            pltpu.VMEM((ctx_moves + 1, 8, rows), F32),
            pltpu.VMEM((ctx_moves, 8, rows), F32),
            dma((4,)),
            dma((2, 4)),
            dma((4, n_head)),
            dma((4, n_head)),
            dma((4, n_head)),
            dma((4, n_head)),
            dma((4,)),
            dma((4,)),
            dma((n_head,)),
            dma((n_head,)),
            dma((ctx_moves,)),
            dma((ctx_moves,)),
        ],
        compiler_params=pltpu.CompilerParams(
            collective_id=0, has_side_effects=True, vmem_limit_bytes=60 * 2**20
        ),
    )(
        queries, keys_base, values_base, grad_out,
        key_dir.reshape(n_head, HEAD_DIM), value_dir.reshape(n_head, HEAD_DIM),
        rewards.reshape(1, rows), episode_end.reshape(1, rows),
    )
    return pl.pallas_call(
        hand_over,
        out_shape=[jax.ShapeDtypeStruct((rows, features), BF16)] * 4,
        in_specs=[hbm] * 4,
        out_specs=[hbm] * 4,
        scratch_shapes=[pltpu.VMEM((4, rows, features), BF16), dma((4, PIECES)), dma((4, PIECES))],
        compiler_params=pltpu.CompilerParams(vmem_limit_bytes=60 * 2**20),
    )(*results)


def solution(mesh):
    wide = P(("ctx", "head"), None)
    steps = P(("ctx", "head"))
    return jax.shard_map(
        on_device,
        mesh=mesh,
        in_specs=(wide, wide, wide, wide, P(), P(), steps, steps),
        out_specs=(wide, wide, wide, wide),
        check_vma=False,
    )
```
